32 devices in a mesh: uvrow: 4 (over z), chan: 2 (over y), tm: 4 (over x, core).
Axes of the slice: x: 2, y: 2, z: 4, core: 2. Of those that a mesh axis runs over, the one named last changes fastest.
Arguments:
- residual_visibility: float32 [2, 32, 128, 8192], P(None, 'tm', 'chan', 'uvrow'), may hold values from -6 to 6
- noise_weight: float32 [32, 128, 8192], P('tm', 'chan', 'uvrow'), may hold values from 0.2 to 5
- uv_tile: int32 [8192, 1], P('uvrow'), may hold values from 0 to 15; in each aligned block of 2048 rows (0 to 2047, 2048 to 4095, ...) at most 256 rows name the same one
- row_offset: int32 [8192], P('uvrow'), may hold values from 0 to 15
- col_offset: int32 [8192], P('uvrow'), may hold values from 0 to 255
- kernel_u: float32 [8, 8192], P(None, 'uvrow'), may hold values from 0.1 to 1
- kernel_v: float32 [8, 8192], P(None, 'uvrow'), may hold values from 0.1 to 1
- sky_model: float32 [128, 256, 256], P('chan', ('uvrow', 'tm')), may hold values from -6 to 6
- prior_precision: float32 [128, 256, 256], P('chan', ('uvrow', 'tm')), may hold values from 0.1 to 3
Outputs:
- gradient: float32 [128, 256, 256], P('chan', ('uvrow', 'tm'))
The draws below stay inside these ranges and needn't reach their ends.
Inputs may be any that keep to these rules, and one draw needn't show every extreme that they name: `uv_tile`: among the 2048 baselines of one index of uvrow (an aligned block), at most 256 name the same tile, a bound that some block reaches.
All inputs are finite; a program needn't handle non-finite values.
Results may differ from the reference program's by a relative error of at most 0.000064.
Values sent between devices are 32-bit elements; how exact they have to be, the bound alone decides.
A program may use at most 64 MiB of HBM per device.

```python
import math
import jax
import jax.numpy as jnp
import numpy as np
from jax import lax

NU = 256
NV = 256
KER = 8
CH_DEV = 64
BL_DEV = 2048
TIMES = 32
FCH = 128
NB = 8192
NTILES = 16
TILE_ROWS = 16
CAP = 256


def touch_ends(entries, key, low, high):
    index_at = [jax.random.randint(jax.random.fold_in(key, axis), (), 0, length) for axis, length in enumerate(entries.shape)]
    widest = entries.shape.index(max(entries.shape))
    next_to = index_at[:widest] + [(index_at[widest] + 1) % entries.shape[widest]] + index_at[widest + 1:]
    return entries.at[tuple(index_at)].set(low).at[tuple(next_to)].set(high)


def block_levels(rng, dims, shards, low, high):
    factor_of = 1.0
    for axis_at, parts in shards:
        draws = jax.random.uniform(jax.random.fold_in(jax.random.fold_in(rng, 6), axis_at), (parts,), jnp.float32, low / len(shards), high / len(shards))
        factor_of = factor_of * jnp.repeat(jnp.exp(draws), dims[axis_at] // parts).reshape((-1,) + (1,) * (len(dims) - 1 - axis_at))
    return factor_of


def routed_block(own_key, own, number, rows, number_of, top, most, slope):
    order = jax.random.permutation(own_key, number_of)
    crowded, usual = load_shares(number_of, rows * top, most, slope, True), load_shares(number_of, rows * top, most, slope, False)
    places = jnp.arange(number_of)

    def named(lengths, turn):
        used = int((lengths > 0).sum())
        fixed = max(1, used // 4)
        shifted = fixed + (places - fixed + turn * (used - fixed)) % max(1, number_of - fixed)
        return jnp.zeros((number_of,), jnp.int32).at[order[jnp.where(places < fixed, places, shifted)]].set(jnp.asarray(lengths, jnp.int32))

    lengths = jnp.where(number % 4 == 0, named(crowded, number // 4), named(usual, number - number // 4 - 1))
    mixed = jax.random.permutation(jax.random.fold_in(own, 3), number_of)
    source_of, sink = mixed[0:number_of // 2 * 2:2], mixed[1:number_of // 2 * 2:2]
    margin = jnp.minimum(lengths[source_of] - 1, most - lengths[sink]) // 2
    margin = jnp.where((source_of == order[0]) | (sink == order[0]) | (lengths[sink] == 0), 0, jnp.maximum(margin, 0))
    shifted = jax.random.randint(jax.random.fold_in(own, 4), (number_of // 2,), 0, 1 << 20) % (margin + 1)
    lengths = lengths.at[source_of].add(-shifted).at[sink].add(shifted)
    labels = jnp.searchsorted(jnp.cumsum(lengths), jnp.arange(rows * top), side="right").astype(jnp.int32)
    grid = labels.reshape(top, rows).T
    grid = grid[jax.random.permutation(jax.random.fold_in(own, 1), rows)]
    turn = jax.random.randint(jax.random.fold_in(own, 2), (rows, 1), 0, top)
    return jnp.take_along_axis(grid, (jnp.arange(top)[None, :] + turn) % top, axis=1)


def load_shares(amount, total, most, skew, full):
    loads = [(1 << 20) // math.isqrt(grade ** skew) + 1 for grade in range(1, amount + 1)]
    largest = most if full else min(most, max(-(-total // amount), total * loads[0] // sum(loads)))
    least = 1 if total - largest >= amount - 1 else 0
    holding, surplus = [largest] + [least] * (amount - 1), total - largest - least * (amount - 1)
    while surplus > 0:
        free = [i for i in range(1, amount) if holding[i] < largest] or [i for i in range(1, amount) if holding[i] < most]
        pool, left = sum([loads[i] for i in free]), surplus
        for i in free:
            more = min(most - holding[i], max(1, left * loads[i] // pool), surplus)
            holding[i] = holding[i] + more
            surplus = surplus - more
    return np.array(holding)


def normal_values(key, shape, spread, bound, split=(), kind=jnp.bfloat16):
    gain = block_levels(key, shape, split, -0.22, 0.18) if split else 1.0
    result = jax.random.normal(key, shape, jnp.float32) * spread * gain
    return jnp.minimum(jnp.maximum(result, -bound), bound).astype(kind)


def setup_inputs(seed: int = 0) -> dict:
    splits = jax.random.split(jax.random.key(seed), 10)
    residual_visibility = normal_values(splits[0], (2, TIMES, FCH, NB), 1.0, 6.0, ((1, 4), (2, 2), (3, 4)), jnp.float32)
    noise_weight = jnp.clip(jnp.exp(math.log(5.0) - 3.218876 * jax.random.uniform(splits[1], (TIMES, FCH, NB), jnp.float32) ** block_levels(splits[1], (TIMES, FCH, NB), ((0, 4), (1, 2), (2, 4)), -0.2, 0.2)), 0.2, 5.0)
    uv_tile_keys = jax.random.split(jax.random.fold_in(splits[2], 1), NB // BL_DEV)
    uv_tile_turns = jax.random.permutation(jax.random.fold_in(splits[2], 3), NB // BL_DEV)
    uv_tile = jax.vmap(lambda own, number: routed_block(jax.random.fold_in(splits[2], 2), own, number, BL_DEV, NTILES, 1, CAP, 2))(uv_tile_keys, uv_tile_turns).reshape((NB, 1))
    row_offset = touch_ends(jax.random.randint(splits[3], (NB,), 0, TILE_ROWS), jax.random.fold_in(splits[3], 1), 0, TILE_ROWS - 1).astype(jnp.int32)
    col_offset = touch_ends(jax.random.randint(splits[4], (NB,), 0, NV), jax.random.fold_in(splits[4], 1), 0, NV - 1).astype(jnp.int32)
    kernel_u = jnp.clip(0.1 + 0.9 * jax.random.uniform(splits[5], (KER, NB), jnp.float32) ** block_levels(splits[5], (KER, NB), ((1, 4),), -0.2, 0.2), 0.1, 1.0)
    kernel_v = jnp.clip(0.1 + 0.9 * jax.random.uniform(splits[6], (KER, NB), jnp.float32) ** block_levels(splits[6], (KER, NB), ((1, 4),), -0.2, 0.2), 0.1, 1.0)
    sky_model = normal_values(splits[7], (FCH, NV, NU), 1.0, 6.0, ((0, 2), (1, 16)), jnp.float32)
    prior_precision = jnp.clip(jnp.exp(math.log(3.0) - 3.4011974 * jax.random.uniform(splits[8], (FCH, NV, NU), jnp.float32) ** block_levels(splits[8], (FCH, NV, NU), ((0, 2), (1, 16)), -0.2, 0.2)), 0.1, 3.0)
    return {"residual_visibility": residual_visibility, "noise_weight": noise_weight, "uv_tile": uv_tile, "row_offset": row_offset, "col_offset": col_offset, "kernel_u": kernel_u, "kernel_v": kernel_v, "sky_model": sky_model, "prior_precision": prior_precision}


def reference(residual_visibility, noise_weight, uv_tile, row_offset, col_offset, kernel_u, kernel_v, sky_model, prior_precision):
    visibility_scale = 1.0 / (KER * math.sqrt(TIMES * NB))
    vis_sum = lax.optimization_barrier(jnp.sum(residual_visibility * noise_weight[None], axis=1)) * visibility_scale
    row_start = (uv_tile[:, 0] * TILE_ROWS + row_offset).astype(jnp.int32)
    kernel_steps = jnp.arange(KER, dtype=jnp.int32)
    grid_rows = (row_start[:, None] + kernel_steps[None, :]) % NU
    grid_cols = (col_offset[:, None] + kernel_steps[None, :]) % NV
    cell_index = (grid_rows[:, :, None] * NV + grid_cols[:, None, :]).reshape(-1).astype(jnp.int32)
    weights = (kernel_u.T[:, :, None] * kernel_v.T[:, None, :]).reshape(NB, KER * KER)
    block_len = math.gcd(CH_DEV, 16)
    blocks = jnp.transpose(vis_sum.reshape(2, FCH // block_len, block_len, NB), (1, 0, 2, 3))

    def one_block(chan_block):
        term_rows = chan_block[:, :, :, None] * weights[None, None]
        term_rows = term_rows.reshape(2 * block_len, NB * KER * KER).T
        uv_grid = jax.ops.segment_sum(term_rows, cell_index, num_segments=NU * NV)
        uv_grid = uv_grid.T.reshape(2, block_len, NU, NV)
        spectrum = jnp.fft.ifft2(lax.complex(uv_grid[0], uv_grid[1]), axes=(1, 2)) * (NU * NV)
        return jnp.transpose(jnp.real(spectrum), (0, 2, 1)).astype(jnp.float32)
    sky_image = lax.map(one_block, blocks).reshape(FCH, NV, NU)
    return sky_image - prior_precision * sky_model
```

```python
import functools
import math

import jax
import jax.numpy as jnp
import numpy as np
from jax import lax
from jax.experimental import pallas as pl
from jax.experimental.pallas import tpu as pltpu
from jax.sharding import PartitionSpec as P

NU = 256
NV = 256
KER = 8
PAD = 8
HALF = NU // 2 + 2 * PAD
MESH = pl.DeviceIdType.MESH


def split3(table, axis):
    high = table.astype(jnp.bfloat16)
    low = (table - high.astype(np.float64)).astype(jnp.bfloat16)
    return np.concatenate([high, high, low], axis=axis)


def tables():
    rows = np.arange(HALF) - PAD
    modes = np.arange(NU)
    angle_u = 2.0 * np.pi / NU * ((modes[:, None] * rows[None, :]) % NU)
    cos_u, sin_u = np.cos(angle_u), np.sin(angle_u)
    table_u = np.concatenate(
        [np.concatenate([cos_u, -sin_u], 1), np.concatenate([sin_u, cos_u], 1)], 0
    )
    angle_v = 2.0 * np.pi / NV * ((np.arange(NV)[:, None] * np.arange(NV)[None, :]) % NV)
    table_v = np.concatenate([np.cos(angle_v), -np.sin(angle_v)], 1)
    return split3(table_u, 1), split3(table_v, 1)


def parts(values):
    high = values.astype(jnp.bfloat16)
    return high, (values - high.astype(jnp.float32)).astype(jnp.bfloat16)


def sum_kernel(own, scale, res_ref, weight_ref, out_ref):
    total = [res_ref[p, 0] * weight_ref[0] for p in range(2)]
    for t in range(1, res_ref.shape[1]):
        weight = weight_ref[t]
        total = [total[p] + res_ref[p, t] * weight for p in range(2)]
    for j in range(out_ref.shape[0]):
        for p in range(2):
            out_ref[j, p * own : (p + 1) * own] = total[p][j * own : (j + 1) * own] * scale


def gather_kernel(
    nz, nt, part_ref, kern_ref, off_ref, vis_ref, kern_out, off_out, got, red,
    s1, r1, s2, r2, sk, rk, so, ro, local_sem,
):
    z = lax.axis_index("uvrow")
    q = lax.axis_index("tm")
    barrier = pltpu.get_barrier_semaphore()
    z_peers = [lax.rem(z + i, nz) for i in range(1, nz)]
    q_peers = [lax.rem(q + i, nt) for i in range(1, nt)]
    for peer in q_peers:
        pl.semaphore_signal(barrier, inc=1, device_id={"tm": peer}, device_id_type=MESH)
    for peer in z_peers:
        pl.semaphore_signal(barrier, inc=1, device_id={"uvrow": peer}, device_id_type=MESH)
    pl.semaphore_wait(barrier, nz + nt - 2)

    first = []
    for i, peer in enumerate(q_peers):
        copy = pltpu.make_async_remote_copy(
            part_ref.at[:, peer], got.at[i], s1.at[i], r1.at[i],
            device_id={"tm": peer}, device_id_type=MESH,
        )
        copy.start()
        first.append(copy)
    second = []
    for i, peer in enumerate(z_peers):
        for src, dst, s, r in ((kern_ref, kern_out, sk, rk), (off_ref, off_out, so, ro)):
            copy = pltpu.make_async_remote_copy(
                src, dst.at[z], s.at[i], r.at[i], device_id={"uvrow": peer}, device_id_type=MESH
            )
            copy.start()
            second.append(copy)
    own = [
        pltpu.make_async_copy(kern_ref, kern_out.at[z], local_sem.at[0]),
        pltpu.make_async_copy(off_ref, off_out.at[z], local_sem.at[1]),
    ]
    for copy in own:
        copy.start()
    for copy in first:
        copy.wait()
    for i in range(nz):
        total = part_ref[i, q]
        for j in range(nt - 1):
            total = total + got[j, i]
        red[i] = total
    for i, peer in enumerate(z_peers):
        copy = pltpu.make_async_remote_copy(
            red.at[peer], vis_ref.at[z], s2.at[i], r2.at[i],
            device_id={"uvrow": peer}, device_id_type=MESH,
        )
        copy.start()
        second.append(copy)
    mine = pltpu.make_async_copy(red.at[z], vis_ref.at[z], local_sem.at[2])
    mine.start()
    own.append(mine)
    for copy in own + second:
        copy.wait()


def grid_kernel(own, vis_ref, kern_ref, off_ref, tu_ref, tv_ref, out_ref, acc, wide, cols):
    step = pl.program_id(0)
    length = vis_ref.shape[2]

    @pl.when(step == 0)
    def _():
        acc[...] = jnp.zeros_like(acc)

    start = off_ref[0, 0:1, :]
    column = off_ref[0, 1:2, :]
    flipped = start >= NU // 2
    sign = jnp.where(flipped, -1, 1)
    start = jnp.where(flipped, start - NU, start)

    def taps(offset, kernel, count, first):
        lane8 = lax.broadcasted_iota(jnp.int32, (KER, length), 0)
        index = (sign * lane8 - offset) & (KER - 1)
        turned = jnp.zeros((KER, length), jnp.float32)
        for j in range(KER):
            turned = jnp.where(index == j, kernel[j : j + 1], turned)
        place = lax.broadcasted_iota(jnp.int32, (count, length), 0) + first
        return jnp.concatenate([turned] * (count // KER), axis=0), sign * place - offset

    v_values, v_tap = taps(column, kern_ref[0, KER:, :], NV, 0)
    v_high, v_low = parts(jnp.where((v_tap & (NV - 1)) < KER, v_values, 0.0))
    cols[:, :length] = v_high
    cols[:, length : 2 * length] = v_low
    cols[:, 2 * length :] = v_high
    u_values, u_tap = taps(start, kern_ref[0, :KER, :], HALF, -PAD)
    u_table = jnp.where((u_tap >= 0) & (u_tap < KER), u_values, 0.0)
    real_sign = sign.astype(jnp.float32)
    for k in range(2 * own):
        row = vis_ref[0, k : k + 1, :]
        if k >= own:
            row = row * real_sign
        high, low = parts(u_table * row)
        at = slice(k * HALF, (k + 1) * HALF)
        wide[at, :length] = high
        wide[at, length : 2 * length] = high
        wide[at, 2 * length :] = low
    acc[...] += lax.dot_general(
        wide[...], cols[...], (((1,), (1,)), ((), ())), preferred_element_type=jnp.float32
    )

    @pl.when(step == pl.num_programs(0) - 1)
    def _():
        for f in range(own):
            both = jnp.concatenate(
                [acc[f * HALF : (f + 1) * HALF], acc[(own + f) * HALF : (own + f + 1) * HALF]], axis=0
            )
            high, low = parts(both)
            turned = jnp.dot(
                tu_ref[...],
                jnp.concatenate([high, low, high], axis=0),
                preferred_element_type=jnp.float32,
            )
            high, low = parts(jnp.concatenate([turned[:NU], turned[NU:]], axis=1))
            out_ref[f] = lax.dot_general(
                tv_ref[...],
                jnp.concatenate([high, low, high], axis=1),
                (((1,), (1,)), ((), ())),
                preferred_element_type=jnp.float32,
            )


def spread_kernel(nz, nt, own, image_ref, sky_ref, prior_ref, out_ref, got, send, recv, local_sem):
    z = lax.axis_index("uvrow")
    q = lax.axis_index("tm")
    count = nz * nt
    me = z * nt + q
    modes = NV // count
    barrier = pltpu.get_barrier_semaphore()

    def place(i):
        peer = lax.rem(me + i, count)
        return peer, {"uvrow": peer // nt, "tm": lax.rem(peer, nt)}

    for i in range(1, count):
        _, device = place(i)
        pl.semaphore_signal(barrier, inc=1, device_id=device, device_id_type=MESH)
    pl.semaphore_wait(barrier, count - 1)
    copies = []
    for i in range(1, count):
        peer, device = place(i)
        copy = pltpu.make_async_remote_copy(
            image_ref.at[:, pl.ds(peer * modes, modes)], got.at[pl.ds(me * own, own)],
            send.at[i], recv.at[i], device_id=device, device_id_type=MESH,
        )
        copy.start()
        copies.append(copy)
    mine = pltpu.make_async_copy(
        image_ref.at[:, pl.ds(me * modes, modes)], got.at[pl.ds(me * own, own)], local_sem
    )
    mine.start()
    mine.wait()
    for copy in copies:
        copy.wait()
    out_ref[...] = got[...] - prior_ref[...] * sky_ref[...]


def body(
    residual_visibility,
    noise_weight,
    uv_tile,
    row_offset,
    col_offset,
    kernel_u,
    kernel_v,
    sky_model,
    prior_precision,
):
    nz = lax.axis_size("uvrow")
    nt = lax.axis_size("tm")
    count = nz * nt
    times = residual_visibility.shape[1]
    channels = residual_visibility.shape[2]
    length = residual_visibility.shape[3]
    own = channels // count
    scale = 1.0 / (KER * math.sqrt(times * nt * length * nz))
    f32 = jnp.float32
    vmem = pl.BlockSpec(memory_space=pltpu.VMEM)
    rows = 8
    limit = 50 * 1024 * 1024

    partial = pl.pallas_call(
        functools.partial(sum_kernel, own, scale),
        grid=(channels // rows,),
        in_specs=[
            pl.BlockSpec((2, times, rows, length), lambda i: (0, 0, i, 0)),
            pl.BlockSpec((times, rows, length), lambda i: (0, i, 0)),
        ],
        out_specs=pl.BlockSpec((rows // own, 2 * own, length), lambda i: (i, 0, 0)),
        out_shape=jax.ShapeDtypeStruct((count, 2 * own, length), f32),
        compiler_params=pltpu.CompilerParams(vmem_limit_bytes=limit),
    )(residual_visibility, noise_weight)

    kernels = jnp.concatenate([kernel_u, kernel_v], axis=0)
    offsets = jnp.stack([uv_tile[:, 0] * (NU // count) + row_offset, col_offset])
    dma = pltpu.SemaphoreType.DMA
    vis, kern_all, off_all = pl.pallas_call(
        functools.partial(gather_kernel, nz, nt),
        in_specs=[vmem] * 3,
        out_specs=[vmem] * 3,
        out_shape=[
            jax.ShapeDtypeStruct((nz, 2 * own, length), f32),
            jax.ShapeDtypeStruct((nz, 2 * KER, length), f32),
            jax.ShapeDtypeStruct((nz, 2, length), jnp.int32),
        ],
        scratch_shapes=[
            pltpu.VMEM((nt - 1, nz, 2 * own, length), f32),
            pltpu.VMEM((nz, 2 * own, length), f32),
            dma((nt - 1,)), dma((nt - 1,)),
            dma((nz - 1,)), dma((nz - 1,)),
            dma((nz - 1,)), dma((nz - 1,)),
            dma((nz - 1,)), dma((nz - 1,)),
            dma((3,)),
        ],
        compiler_params=pltpu.CompilerParams(
            collective_id=0, has_side_effects=True, vmem_limit_bytes=limit
        ),
    )(partial.reshape(nz, nt, 2 * own, length), kernels, offsets)

    chunk = min(512, length)
    per = length // chunk
    table_u, table_v = tables()
    image = pl.pallas_call(
        functools.partial(grid_kernel, own),
        grid=(nz * per,),
        in_specs=[
            pl.BlockSpec((1, 2 * own, chunk), lambda i: (i // per, 0, i % per)),
            pl.BlockSpec((1, 2 * KER, chunk), lambda i: (i // per, 0, i % per)),
            pl.BlockSpec((1, 2, chunk), lambda i: (i // per, 0, i % per)),
            vmem,
            vmem,
        ],
        out_specs=pl.BlockSpec((own, NV, NU), lambda i: (0, 0, 0)),
        out_shape=jax.ShapeDtypeStruct((own, NV, NU), f32),
        scratch_shapes=[
            pltpu.VMEM((2 * own * HALF, NV), f32),
            pltpu.VMEM((2 * own * HALF, 3 * chunk), jnp.bfloat16),
            pltpu.VMEM((NV, 3 * chunk), jnp.bfloat16),
        ],
        compiler_params=pltpu.CompilerParams(vmem_limit_bytes=limit),
    )(vis, kern_all, off_all, jnp.asarray(table_u), jnp.asarray(table_v))

    return pl.pallas_call(
        functools.partial(spread_kernel, nz, nt, own),
        in_specs=[vmem] * 3,
        out_specs=vmem,
        out_shape=jax.ShapeDtypeStruct(sky_model.shape, f32),
        scratch_shapes=[
            pltpu.VMEM(sky_model.shape, f32),
            dma((count,)), dma((count,)), dma,
        ],
        compiler_params=pltpu.CompilerParams(
            collective_id=1, has_side_effects=True, vmem_limit_bytes=limit
        ),
    )(image, sky_model, prior_precision)


def solution(mesh):
    return jax.shard_map(
        body,
        mesh=mesh,
        in_specs=(
            P(None, "tm", "chan", "uvrow"),
            P("tm", "chan", "uvrow"),
            P("uvrow", None),
            P("uvrow"),
            P("uvrow"),
            P(None, "uvrow"),
            P(None, "uvrow"),
            P("chan", ("uvrow", "tm"), None),
            P("chan", ("uvrow", "tm"), None),
        ),
        out_specs=P("chan", ("uvrow", "tm"), None),
        check_vma=False,
    )
```

```python
import functools
import math

import jax
import jax.numpy as jnp
import numpy as np
from jax import lax
from jax.experimental import pallas as pl
from jax.experimental.pallas import tpu as pltpu
from jax.sharding import PartitionSpec as P

NU = 256
NV = 256
KER = 8
PAD = 8
HALF = NU // 2 + 2 * PAD
MESH = pl.DeviceIdType.MESH


def split3(table, axis):
    high = table.astype(jnp.bfloat16)
    low = (table - high.astype(np.float64)).astype(jnp.bfloat16)
    return np.concatenate([high, high, low], axis=axis)


def tables():
    rows = np.arange(HALF) - PAD
    modes = np.arange(NU)
    angle_u = 2.0 * np.pi / NU * ((modes[:, None] * rows[None, :]) % NU)
    cos_u, sin_u = np.cos(angle_u), np.sin(angle_u)
    table_u = np.concatenate(
        [np.concatenate([cos_u, -sin_u], 1), np.concatenate([sin_u, cos_u], 1)], 0
    )
    angle_v = 2.0 * np.pi / NV * ((np.arange(NV)[:, None] * np.arange(NV)[None, :]) % NV)
    table_v = np.concatenate([np.cos(angle_v), -np.sin(angle_v)], 1)
    return split3(table_u, 1), split3(table_v, 1)


def parts(values):
    high = values.astype(jnp.bfloat16)
    return high, (values - high.astype(jnp.float32)).astype(jnp.bfloat16)


def taps(offset, sign, kernel, count, first):
    length = offset.shape[1]
    lane8 = lax.broadcasted_iota(jnp.int32, (KER, length), 0)
    index = (sign * lane8 - offset) & (KER - 1)
    turned = jnp.zeros((KER, length), jnp.float32)
    for j in range(KER):
        turned = jnp.where(index == j, kernel[j : j + 1], turned)
    place = lax.broadcasted_iota(jnp.int32, (count, length), 0) + first
    return jnp.concatenate([turned] * (count // KER), axis=0), sign * place - offset


def fit_kernel(
    nz, nt, own, chunk, scale,
    res_hbm, weight_hbm, ku_ref, kv_ref, tile_ref, row_ref, col_ref, tu_ref, tv_ref,
    out_ref,
    res, weight, part, got_a, got_b, mixed, vis, ku, kv, off, rows, cols, wide_a, wide_b, acc, image,
    load_sem, send_a, recv_a, send_b, recv_b, send_c, recv_c, send_k, recv_k, send_o, recv_o, send_i, recv_i, local_sem,
):
    z = lax.axis_index("uvrow")
    q = lax.axis_index("tm")
    half = nt // 2
    high, core = q // 2, lax.rem(q, 2)
    count = nz * nt
    me = z * nt + q
    modes = NV // count
    length = res.shape[3]
    per = length // chunk
    chunks = nz * per
    group = 8
    per_z = nt * own // group
    pairs = group // (2 * own)
    at_z = [lax.rem(z + 1 + k, nz) for k in range(nz)]

    loads = []
    for n in range(nz * per_z):
        first = pl.multiple_of((at_z[n // per_z] * per_z + n % per_z) * group, group)
        at = pl.ds(first, group)
        pair = [
            pltpu.make_async_copy(res_hbm.at[:, :, at], res.at[:, :, pl.ds(n * group, group)], load_sem.at[n, 0]),
            pltpu.make_async_copy(weight_hbm.at[:, at], weight.at[:, pl.ds(n * group, group)], load_sem.at[n, 1]),
        ]
        for copy in pair:
            copy.start()
        loads.append(pair)

    def device(i):
        peer = lax.rem(me + i, count)
        return peer, {"uvrow": peer // nt, "tm": lax.rem(peer, nt)}

    barrier = pltpu.get_barrier_semaphore()
    for i in range(1, count):
        pl.semaphore_signal(barrier, inc=1, device_id=device(i)[1], device_id_type=MESH)
    off[z, 0:1] = tile_ref[...] * (NU // count) + row_ref[...]
    off[z, 1:2] = col_ref[...]
    ku[z] = ku_ref[...]
    kv[z] = kv_ref[...]
    pl.semaphore_wait(barrier, count - 1)

    def to_z(k, source, target, send, recv):
        return pltpu.make_async_remote_copy(
            source, target, send, recv, device_id={"uvrow": at_z[k]}, device_id_type=MESH
        )

    kernels = []
    for k in range(nz - 1):
        kernels.append(
            [
                to_z(k, off.at[z], off.at[z], send_o.at[k], recv_o.at[k]),
                to_z(k, ku.at[z], ku.at[z], send_k.at[k, 0], recv_k.at[k, 0]),
                to_z(k, kv.at[z], kv.at[z], send_k.at[k, 1], recv_k.at[k, 1]),
            ]
        )
        for copy in kernels[k]:
            copy.start()

    halves = []
    for n in range(nz * per_z):
        for copy in loads[n]:
            copy.wait()
        at = slice(n * group, (n + 1) * group)
        total = [res[p, 0, at] * weight[0, at] for p in range(2)]
        for t in range(1, res.shape[1]):
            total = [total[p] + res[p, t, at] * weight[t, at] for p in range(2)]
        for j in range(2 * pairs):
            for p in range(2):
                part[n * pairs + j // 2, j % 2, p * own : (p + 1) * own] = (
                    total[p][j * own : (j + 1) * own] * scale
                )
        where = pl.ds(n * pairs, pairs)
        copy = pltpu.make_async_remote_copy(
            part.at[where, 1 - core], got_a.at[where], send_a.at[n], recv_a.at[n],
            device_id={"tm": high * 2 + 1 - core}, device_id_type=MESH,
        )
        copy.start()
        halves.append(copy)

    quarters = []
    for k in range(nz):
        for s in range(per_z):
            halves[k * per_z + s].wait()
        for h in range(half):
            mixed[k, h] = part[k * half + h, core] + got_a[k * half + h]
        for i in range(1, half):
            to = lax.rem(high + i, half)
            copy = pltpu.make_async_remote_copy(
                mixed.at[k, to], got_b.at[k, i - 1], send_b.at[k, i - 1], recv_b.at[k, i - 1],
                device_id={"tm": to * 2 + core}, device_id_type=MESH,
            )
            copy.start()
            quarters.append(copy)

    def tabulate(at):
        def one(k, carry):
            lanes = pl.ds(pl.multiple_of(k * chunk, chunk), chunk)
            start = off[at, 0:1, lanes]
            column = off[at, 1:2, lanes]
            flipped = start >= NU // 2
            sign = jnp.where(flipped, -1, 1)
            start = jnp.where(flipped, start - NU, start)
            values, tap = taps(column, sign, kv[at, :, lanes], NV, 0)
            v_high, v_low = parts(jnp.where((tap & (NV - 1)) < KER, values, 0.0))
            n = at * per + k
            cols[n, :, :chunk] = v_high
            cols[n, :, chunk : 2 * chunk] = v_low
            cols[n, :, 2 * chunk :] = v_high
            values, tap = taps(start, sign, ku[at, :, lanes], HALF, -PAD)
            rows[n] = jnp.where((tap >= 0) & (tap < KER), values, 0.0)
            return carry

        lax.fori_loop(0, per, one, 0)

    tabulate(z)
    blocks = []
    for k in range(nz):
        for i in range(half - 1):
            quarters[k * (half - 1) + i].wait()
        total = mixed[k, high]
        for i in range(half - 1):
            total = total + got_b[k, i]
        if k == nz - 1:
            vis[z] = total
            continue
        part[k, 0] = total
        copy = to_z(k, part.at[k, 0], vis.at[z], send_c.at[k], recv_c.at[k])
        copy.start()
        blocks.append(copy)
    for k in range(nz - 1):
        for copy in kernels[k]:
            copy.wait()
    for k in range(nz - 1):
        tabulate(at_z[k])
    for copy in blocks:
        copy.wait()

    def build(n, wide):
        f, c = n // chunks, lax.rem(n, chunks)
        lanes = pl.ds(pl.multiple_of(lax.rem(c, per) * chunk, chunk), chunk)
        table = rows[c]
        sign = jnp.where(off[c // per, 0:1, lanes] >= NU // 2, -1.0, 1.0)
        for p in range(2):
            row = vis[c // per, pl.ds(p * own + f, 1), lanes]
            if p:
                row = row * sign
            w_high, w_low = parts(table * row)
            at = slice(p * HALF, (p + 1) * HALF)
            wide[at, :chunk] = w_high
            wide[at, chunk : 2 * chunk] = w_high
            wide[at, 2 * chunk :] = w_low

    def product(wide, c):
        return lax.dot_general(
            wide[...], cols[c], (((1,), (1,)), ((), ())), preferred_element_type=jnp.float32
        )

    def send(f, i):
        peer, to = device(i)
        return pltpu.make_async_remote_copy(
            image.at[f, pl.ds(pl.multiple_of(peer * modes, modes), modes)], out_ref.at[me * own + f],
            send_i.at[f, i], recv_i.at[f, i], device_id=to, device_id_type=MESH,
        )

    def keep(f):
        return pltpu.make_async_copy(
            image.at[f, pl.ds(pl.multiple_of(me * modes, modes), modes)], out_ref.at[me * own + f], local_sem.at[f]
        )

    build(0, wide_a)

    def channel(f, carry):
        acc[...] = jnp.zeros_like(acc)

        def two(k, carry):
            n = f * chunks + 2 * k
            build(n + 1, wide_b)
            acc[...] += product(wide_a, 2 * k)
            build(lax.rem(n + 2, own * chunks), wide_a)
            acc[...] += product(wide_b, 2 * k + 1)
            return carry

        lax.fori_loop(0, chunks // 2, two, 0)
        g_high, g_low = parts(acc[...])
        turned = jnp.dot(
            tu_ref[...],
            jnp.concatenate([g_high, g_low, g_high], axis=0),
            preferred_element_type=jnp.float32,
        )
        g_high, g_low = parts(jnp.concatenate([turned[:NU], turned[NU:]], axis=1))
        image[f] = lax.dot_general(
            tv_ref[...],
            jnp.concatenate([g_high, g_low, g_high], axis=1),
            (((1,), (1,)), ((), ())),
            preferred_element_type=jnp.float32,
        )
        for i in range(1, count):
            send(f, i).start()
        keep(f).start()
        return carry

    lax.fori_loop(0, own, channel, 0)

    def finish(f, carry):
        for i in range(1, count):
            send(f, i).wait()
        keep(f).wait()
        return carry

    lax.fori_loop(0, own, finish, 0)


def body(
    residual_visibility,
    noise_weight,
    uv_tile,
    row_offset,
    col_offset,
    kernel_u,
    kernel_v,
    sky_model,
    prior_precision,
):
    nz = lax.axis_size("uvrow")
    nt = lax.axis_size("tm")
    count = nz * nt
    times = residual_visibility.shape[1]
    channels = residual_visibility.shape[2]
    length = residual_visibility.shape[3]
    own = channels // count
    half = nt // 2
    scale = 1.0 / (KER * math.sqrt(times * nt * length * nz))
    f32 = jnp.float32
    bf16 = jnp.bfloat16
    chunk = min(512, length)
    chunks = nz * (length // chunk)
    table_u, table_v = tables()
    dma = pltpu.SemaphoreType.DMA
    vmem = pltpu.VMEM
    in_vmem = pl.BlockSpec(memory_space=pltpu.VMEM)
    in_hbm = pl.BlockSpec(memory_space=pl.ANY)
    groups = channels // 8

    sky_image = pl.pallas_call(
        functools.partial(fit_kernel, nz, nt, own, chunk, scale),
        in_specs=[in_hbm] * 2 + [in_vmem] * 7,
        out_specs=in_hbm,
        out_shape=jax.ShapeDtypeStruct(sky_model.shape, f32),
        scratch_shapes=[
            vmem((2, times, channels, length), f32),
            vmem((times, channels, length), f32),
            vmem((count // 2, 2, 2 * own, length), f32),
            vmem((count // 2, 2 * own, length), f32),
            vmem((nz, half - 1, 2 * own, length), f32),
            vmem((nz, half, 2 * own, length), f32),
            vmem((nz, 2 * own, length), f32),
            vmem((nz, KER, length), f32),
            vmem((nz, KER, length), f32),
            vmem((nz, 2, length), jnp.int32),
            vmem((chunks, HALF, chunk), f32),
            vmem((chunks, NV, 3 * chunk), bf16),
            vmem((2 * HALF, 3 * chunk), bf16),
            vmem((2 * HALF, 3 * chunk), bf16),
            vmem((2 * HALF, NV), f32),
            vmem((own, NV, NU), f32),
            dma((groups, 2)),
            dma((groups,)), dma((groups,)),
            dma((nz, half - 1)), dma((nz, half - 1)),
            dma((nz - 1,)), dma((nz - 1,)),
            dma((nz - 1, 2)), dma((nz - 1, 2)),
            dma((nz - 1,)), dma((nz - 1,)),
            dma((own, count)), dma((own, count)),
            dma((own,)),
        ],
        compiler_params=pltpu.CompilerParams(
            collective_id=0, has_side_effects=True, vmem_limit_bytes=58 * 1024 * 1024
        ),
    )(
        residual_visibility,
        noise_weight,
        kernel_u,
        kernel_v,
        uv_tile.reshape(1, length),
        row_offset.reshape(1, length),
        col_offset.reshape(1, length),
        jnp.asarray(table_u),
        jnp.asarray(table_v),
    )
    return sky_image - prior_precision * sky_model


def solution(mesh):
    return jax.shard_map(
        body,
        mesh=mesh,
        in_specs=(
            P(None, "tm", "chan", "uvrow"),
            P("tm", "chan", "uvrow"),
            P("uvrow", None),
            P("uvrow"),
            P("uvrow"),
            P(None, "uvrow"),
            P(None, "uvrow"),
            P("chan", ("uvrow", "tm"), None),
            P("chan", ("uvrow", "tm"), None),
        ),
        out_specs=P("chan", ("uvrow", "tm"), None),
        check_vma=False,
    )
```

```python
import functools
import math

import jax
import jax.numpy as jnp
import numpy as np
from jax import lax
from jax.experimental import pallas as pl
from jax.experimental.pallas import tpu as pltpu
from jax.sharding import PartitionSpec as P

NU = 256
NV = 256
KER = 8
PAD = 8
HALF = NU // 2 + 2 * PAD
MESH = pl.DeviceIdType.MESH


def split3(table, axis):
    high = table.astype(jnp.bfloat16)
    low = (table - high.astype(np.float64)).astype(jnp.bfloat16)
    return np.concatenate([high, high, low], axis=axis)


def tables():
    rows = np.arange(HALF) - PAD
    modes = np.arange(NU)
    angle_u = 2.0 * np.pi / NU * ((modes[:, None] * rows[None, :]) % NU)
    cos_u, sin_u = np.cos(angle_u), np.sin(angle_u)
    table_u = np.concatenate(
        [np.concatenate([cos_u, -sin_u], 1), np.concatenate([sin_u, cos_u], 1)], 0
    )
    angle_v = 2.0 * np.pi / NV * ((np.arange(NV)[:, None] * np.arange(NV)[None, :]) % NV)
    table_v = np.concatenate([np.cos(angle_v), -np.sin(angle_v)], 1)
    return split3(table_u, 1), split3(table_v, 1)


def parts(values):
    high = values.astype(jnp.bfloat16)
    return high, (values - high.astype(jnp.float32)).astype(jnp.bfloat16)


def taps(offset, sign, kernel, count, first):
    length = offset.shape[1]
    lane8 = lax.broadcasted_iota(jnp.int32, (KER, length), 0)
    index = (sign * lane8 - offset) & (KER - 1)
    turned = jnp.zeros((KER, length), jnp.float32)
    for j in range(KER):
        turned = jnp.where(index == j, kernel[j : j + 1], turned)
    place = lax.broadcasted_iota(jnp.int32, (count, length), 0) + first
    return jnp.concatenate([turned] * (count // KER), axis=0), sign * place - offset


def fit_kernel(
    nz, nt, own, chunk, scale,
    res_hbm, weight_hbm, ku_ref, kv_ref, tile_ref, row_ref, col_ref, tu_ref, tv_ref,
    out_ref,
    res, weight, part, got_a, got_b, mixed, vis, ku, kv, off, rows, cols, wide_a, wide_b, acc, image,
    load_sem, send_a, recv_a, send_b, recv_b, send_c, recv_c, send_k, recv_k, send_o, recv_o, send_i, recv_i, local_sem,
):
    z = lax.axis_index("uvrow")
    q = lax.axis_index("tm")
    half = nt // 2
    high, core = q // 2, lax.rem(q, 2)
    count = nz * nt
    me = z * nt + q
    modes = NV // count
    length = res.shape[3]
    batch = 2 if own % 2 == 0 else 1
    per = length // chunk
    chunks = nz * per
    group = 8
    per_z = nt * own // group
    pairs = group // (2 * own)
    at_z = [lax.rem(z + 1 + k, nz) for k in range(nz)]

    loads = []
    for n in range(nz * per_z):
        first = pl.multiple_of((at_z[n // per_z] * per_z + n % per_z) * group, group)
        at = pl.ds(first, group)
        pair = [
            pltpu.make_async_copy(res_hbm.at[:, :, at], res.at[:, :, pl.ds(n * group, group)], load_sem.at[n, 0]),
            pltpu.make_async_copy(weight_hbm.at[:, at], weight.at[:, pl.ds(n * group, group)], load_sem.at[n, 1]),
        ]
        for copy in pair:
            copy.start()
        loads.append(pair)

    def device(i):
        peer = lax.rem(me + i, count)
        return peer, {"uvrow": peer // nt, "tm": lax.rem(peer, nt)}

    barrier = pltpu.get_barrier_semaphore()
    for i in range(1, count):
        pl.semaphore_signal(barrier, inc=1, device_id=device(i)[1], device_id_type=MESH)
    off[z, 0:1] = tile_ref[...] * (NU // count) + row_ref[...]
    off[z, 1:2] = col_ref[...]
    ku[z] = ku_ref[...]
    kv[z] = kv_ref[...]
    pl.semaphore_wait(barrier, count - 1)

    def to_z(k, source, target, send, recv):
        return pltpu.make_async_remote_copy(
            source, target, send, recv, device_id={"uvrow": at_z[k]}, device_id_type=MESH
        )

    kernels = []
    for k in range(nz - 1):
        kernels.append(
            [
                to_z(k, off.at[z], off.at[z], send_o.at[k], recv_o.at[k]),
                to_z(k, ku.at[z], ku.at[z], send_k.at[k, 0], recv_k.at[k, 0]),
                to_z(k, kv.at[z], kv.at[z], send_k.at[k, 1], recv_k.at[k, 1]),
            ]
        )
        for copy in kernels[k]:
            copy.start()

    halves, quarters, blocks = [], [], []

    def add_times(n):
        for copy in loads[n]:
            copy.wait()
        at = slice(n * group, (n + 1) * group)
        total = [res[p, 0, at] * weight[0, at] for p in range(2)]
        for t in range(1, res.shape[1]):
            total = [total[p] + res[p, t, at] * weight[t, at] for p in range(2)]
        for j in range(2 * pairs):
            for p in range(2):
                part[n * pairs + j // 2, j % 2, p * own : (p + 1) * own] = (
                    total[p][j * own : (j + 1) * own] * scale
                )
        where = pl.ds(n * pairs, pairs)
        copy = pltpu.make_async_remote_copy(
            part.at[where, 1 - core], got_a.at[where], send_a.at[n], recv_a.at[n],
            device_id={"tm": high * 2 + 1 - core}, device_id_type=MESH,
        )
        copy.start()
        halves.append(copy)

    def add_cores(k):
        for s in range(per_z):
            halves[k * per_z + s].wait()
        for h in range(half):
            mixed[k, h] = part[k * half + h, core] + got_a[k * half + h]
        for i in range(1, half):
            to = lax.rem(high + i, half)
            copy = pltpu.make_async_remote_copy(
                mixed.at[k, to], got_b.at[k, i - 1], send_b.at[k, i - 1], recv_b.at[k, i - 1],
                device_id={"tm": to * 2 + core}, device_id_type=MESH,
            )
            copy.start()
            quarters.append(copy)

    def add_chips(k):
        for i in range(half - 1):
            quarters[k * (half - 1) + i].wait()
        total = mixed[k, high]
        for i in range(half - 1):
            total = total + got_b[k, i]
        if k == nz - 1:
            vis[z] = total
            return
        part[k, 0] = total
        copy = to_z(k, part.at[k, 0], vis.at[z], send_c.at[k], recv_c.at[k])
        copy.start()
        blocks.append(copy)

    def tabulate(at):
        def one(k, carry):
            lanes = pl.ds(pl.multiple_of(k * chunk, chunk), chunk)
            start = off[at, 0:1, lanes]
            column = off[at, 1:2, lanes]
            flipped = start >= NU // 2
            sign = jnp.where(flipped, -1, 1)
            start = jnp.where(flipped, start - NU, start)
            values, tap = taps(column, sign, kv[at, :, lanes], NV, 0)
            v_high, v_low = parts(jnp.where((tap & (NV - 1)) < KER, values, 0.0))
            n = at * per + k
            cols[n, :, :chunk] = v_high
            cols[n, :, chunk : 2 * chunk] = v_low
            cols[n, :, 2 * chunk :] = v_high
            values, tap = taps(start, sign, ku[at, :, lanes], HALF, -PAD)
            rows[n] = jnp.where((tap >= 0) & (tap < KER), values, 0.0)
            return carry

        lax.fori_loop(0, per, one, 0)

    for k in range(nz):
        for s in range(per_z):
            add_times(k * per_z + s)
        if k >= 1:
            add_cores(k - 1)
        if k >= 2:
            add_chips(k - 2)
    add_cores(nz - 1)
    add_chips(nz - 2)
    tabulate(z)
    add_chips(nz - 1)
    for k in range(nz - 1):
        for copy in kernels[k]:
            copy.wait()
    for k in range(nz - 1):
        tabulate(at_z[k])
    for copy in blocks:
        copy.wait()

    def build(n, wide):
        f, c = n // chunks * batch, lax.rem(n, chunks)
        lanes = pl.ds(pl.multiple_of(lax.rem(c, per) * chunk, chunk), chunk)
        table = rows[c]
        sign = jnp.where(off[c // per, 0:1, lanes] >= NU // 2, -1.0, 1.0)
        for e in range(2 * batch):
            row = vis[c // per, pl.ds(e % 2 * own + f + e // 2, 1), lanes]
            if e % 2:
                row = row * sign
            w_high, w_low = parts(table * row)
            at = slice(e * HALF, (e + 1) * HALF)
            wide[at, :chunk] = w_high
            wide[at, chunk : 2 * chunk] = w_high
            wide[at, 2 * chunk :] = w_low

    def product(wide, c):
        return lax.dot_general(
            wide[...], cols[c], (((1,), (1,)), ((), ())), preferred_element_type=jnp.float32
        )

    def send(f, i):
        peer, to = device(i)
        return pltpu.make_async_remote_copy(
            image.at[f, pl.ds(pl.multiple_of(peer * modes, modes), modes)], out_ref.at[me * own + f],
            send_i.at[f, i], recv_i.at[f, i], device_id=to, device_id_type=MESH,
        )

    def keep(f):
        return pltpu.make_async_copy(
            image.at[f, pl.ds(pl.multiple_of(me * modes, modes), modes)], out_ref.at[me * own + f], local_sem.at[f]
        )

    build(0, wide_a)

    def channels(g, carry):
        acc[...] = jnp.zeros_like(acc)

        def two(k, carry):
            n = g * chunks + 2 * k
            build(n + 1, wide_b)
            acc[...] += product(wide_a, 2 * k)
            build(lax.rem(n + 2, own // batch * chunks), wide_a)
            acc[...] += product(wide_b, 2 * k + 1)
            return carry

        lax.fori_loop(0, chunks // 2, two, 0)
        for e in range(batch):
            f = g * batch + e
            g_high, g_low = parts(acc[2 * e * HALF : 2 * (e + 1) * HALF])
            turned = jnp.dot(
                tu_ref[...],
                jnp.concatenate([g_high, g_low, g_high], axis=0),
                preferred_element_type=jnp.float32,
            )
            g_high, g_low = parts(jnp.concatenate([turned[:NU], turned[NU:]], axis=1))
            image[f] = lax.dot_general(
                tv_ref[...],
                jnp.concatenate([g_high, g_low, g_high], axis=1),
                (((1,), (1,)), ((), ())),
                preferred_element_type=jnp.float32,
            )
            for i in range(1, count):
                send(f, i).start()
            keep(f).start()
        return carry

    lax.fori_loop(0, own // batch, channels, 0)

    def finish(f, carry):
        for i in range(1, count):
            send(f, i).wait()
        keep(f).wait()
        return carry

    lax.fori_loop(0, own, finish, 0)


def body(
    residual_visibility,
    noise_weight,
    uv_tile,
    row_offset,
    col_offset,
    kernel_u,
    kernel_v,
    sky_model,
    prior_precision,
):
    nz = lax.axis_size("uvrow")
    nt = lax.axis_size("tm")
    count = nz * nt
    times = residual_visibility.shape[1]
    channels = residual_visibility.shape[2]
    length = residual_visibility.shape[3]
    own = channels // count
    half = nt // 2
    batch = 2 if own % 2 == 0 else 1
    scale = 1.0 / (KER * math.sqrt(times * nt * length * nz))
    f32 = jnp.float32
    bf16 = jnp.bfloat16
    chunk = min(512, length)
    chunks = nz * (length // chunk)
    table_u, table_v = tables()
    dma = pltpu.SemaphoreType.DMA
    vmem = pltpu.VMEM
    in_vmem = pl.BlockSpec(memory_space=pltpu.VMEM)
    in_hbm = pl.BlockSpec(memory_space=pl.ANY)
    groups = channels // 8

    sky_image = pl.pallas_call(
        functools.partial(fit_kernel, nz, nt, own, chunk, scale),
        in_specs=[in_hbm] * 2 + [in_vmem] * 7,
        out_specs=in_hbm,
        out_shape=jax.ShapeDtypeStruct(sky_model.shape, f32),
        scratch_shapes=[
            vmem((2, times, channels, length), f32),
            vmem((times, channels, length), f32),
            vmem((count // 2, 2, 2 * own, length), f32),
            vmem((count // 2, 2 * own, length), f32),
            vmem((nz, half - 1, 2 * own, length), f32),
            vmem((nz, half, 2 * own, length), f32),
            vmem((nz, 2 * own, length), f32),
            vmem((nz, KER, length), f32),
            vmem((nz, KER, length), f32),
            vmem((nz, 2, length), jnp.int32),
            vmem((chunks, HALF, chunk), f32),
            vmem((chunks, NV, 3 * chunk), bf16),
            vmem((2 * batch * HALF, 3 * chunk), bf16),
            vmem((2 * batch * HALF, 3 * chunk), bf16),
            vmem((2 * batch * HALF, NV), f32),
            vmem((own, NV, NU), f32),
            dma((groups, 2)),
            dma((groups,)), dma((groups,)),
            dma((nz, half - 1)), dma((nz, half - 1)),
            dma((nz - 1,)), dma((nz - 1,)),
            dma((nz - 1, 2)), dma((nz - 1, 2)),
            dma((nz - 1,)), dma((nz - 1,)),
            dma((own, count)), dma((own, count)),
            dma((own,)),
        ],
        compiler_params=pltpu.CompilerParams(
            collective_id=0, has_side_effects=True, vmem_limit_bytes=58 * 1024 * 1024
        ),
    )(
        residual_visibility,
        noise_weight,
        kernel_u,
        kernel_v,
        uv_tile.reshape(1, length),
        row_offset.reshape(1, length),
        col_offset.reshape(1, length),
        jnp.asarray(table_u),
        jnp.asarray(table_v),
    )
    return sky_image - prior_precision * sky_model


def solution(mesh):
    return jax.shard_map(
        body,
        mesh=mesh,
        in_specs=(
            P(None, "tm", "chan", "uvrow"),
            P("tm", "chan", "uvrow"),
            P("uvrow", None),
            P("uvrow"),
            P("uvrow"),
            P(None, "uvrow"),
            P(None, "uvrow"),
            P("chan", ("uvrow", "tm"), None),
            P("chan", ("uvrow", "tm"), None),
        ),
        out_specs=P("chan", ("uvrow", "tm"), None),
        check_vma=False,
    )
```
